256 devices in a mesh: section: 2 (over x_hi), dp: 8 (over x_lo, y), mp: 16 (over z, core).
Axes of the slice: x: 4 (x_hi: 2, x_lo: 2; x = x_hi * 2 + x_lo), y: 4, z: 8, core: 2. Of those that a mesh axis runs over, the one named last changes fastest.
Arguments:
- handoff: bfloat16 [2, 1024, 12288], P('section', ('mp', 'dp')), may hold values from -44 to 44
- ln_gain: float32 [2, 12288], P('section', 'dp'), may hold values from 0.1 to 1.9
- ln_bias: float32 [2, 12288], P('section', 'dp'), may hold values from -3 to 3
- w_up: bfloat16 [2, 12288, 24576], P('section', 'dp', 'mp'), may hold values from -0.0546875 to 0.0546875
- up_bias: float32 [2, 24576], P('section', 'mp'), may hold values from -3 to 3
- w_down: bfloat16 [2, 24576, 12288], P('section', 'mp', 'dp'), may hold values from -0.0390625 to 0.0390625
- down_bias: float32 [2, 12288], P('section', 'dp'), may hold values from -3 to 3
Outputs:
- layer_out: bfloat16 [2, 1024, 12288], P('section', 'mp', 'dp')
The draws below stay inside these ranges and needn't reach their ends.
All inputs are finite; a program needn't handle non-finite values.
Results may differ from the reference program's by a relative error of at most 0.0034.
Values may be sent and summed in bfloat16 or wider, within the bound.
A program may use at most 64 MiB of HBM per device.

```python
import jax
import jax.numpy as jnp
from jax import lax

D = 12288
FFW = 24576
TOKENS = 1024


def draw_handoff(key, part):
    key = jax.random.fold_in(key, 11)
    key_base, key_cols, key_rows = jax.random.split(key, 3)
    ramp = 0.6 + 1.2 * jnp.arange(D, dtype=jnp.float32) / D
    columns = jnp.exp(jax.random.uniform(key_cols, (2, 1, D), jnp.float32, jnp.log(0.3), jnp.log(3.0)))
    rows = jnp.exp(jax.random.uniform(key_rows, (2, TOKENS, 1), jnp.float32, jnp.log(0.2), jnp.log(2.0)))
    base = jax.random.normal(key_base, (2, TOKENS, D), jnp.float32)
    base = jnp.clip(base, -4.0, 4.0)
    return (base * rows * columns * ramp).astype(jnp.bfloat16)


def block_scale(rng, dims, cuts, least, top_value):
    factor_of, own = 1.0, jax.random.fold_in(rng, 6)
    for axis_at, shards_of in cuts:
        draws = jnp.exp(jax.random.uniform(jax.random.fold_in(own, axis_at), (shards_of,), jnp.float32, least / len(cuts), top_value / len(cuts)))
        factor_of = factor_of * jnp.repeat(draws, dims[axis_at] // shards_of).reshape([-1 if axis == axis_at else 1 for axis in range(len(dims))])
    return factor_of


def scatter_about(key, shape, width, limit, cuts=(), held_as=jnp.bfloat16):
    values = width * jax.random.normal(key, shape, jnp.float32)
    if cuts:
        values = values * block_scale(key, shape, cuts, -0.22, 0.18)
    return jnp.clip(values, -limit, limit).astype(held_as)


def setup_inputs(seed: int = 0) -> dict:
    streams_of = jax.random.split(jax.random.key(seed), 8)
    handoff = draw_handoff(jax.random.fold_in(streams_of[7], 71), 0)
    ln_gain = jnp.clip(1.0 + 0.18 * jax.random.normal(streams_of[1], (2, D), jnp.float32), 0.1, 1.9)
    ln_bias = scatter_about(streams_of[2], (2, D), 0.5, 3.0, ((0, 2), (1, 8)), jnp.float32)
    w_up = scatter_about(streams_of[3], (2, D, FFW), D ** -0.5, 0.0546875, ((0, 2), (1, 8), (2, 16)))
    up_bias = scatter_about(streams_of[4], (2, FFW), 0.5, 3.0, ((0, 2), (1, 16)), jnp.float32)
    w_down = scatter_about(streams_of[5], (2, FFW, D), FFW ** -0.5, 0.0390625, ((0, 2), (1, 16), (2, 8)))
    down_bias = scatter_about(streams_of[6], (2, D), 0.5, 3.0, ((0, 2), (1, 8)), jnp.float32)
    return {"handoff": handoff, "ln_gain": ln_gain, "ln_bias": ln_bias, "w_up": w_up, "up_bias": up_bias, "w_down": w_down, "down_bias": down_bias}


def section_block(x, gain, shift, w_up, up_bias, w_down, down_bias):
    mean = lax.optimization_barrier(jnp.mean(x, axis=1, keepdims=True))
    centered = x - mean
    var = lax.optimization_barrier(jnp.mean(centered * centered, axis=1, keepdims=True))
    normed = (centered * lax.rsqrt(var + 1e-05) * gain + shift).astype(jnp.bfloat16)
    pre = jnp.dot(normed, w_up, preferred_element_type=jnp.float32) + up_bias
    hidden = jnp.maximum(pre, 0.0).astype(jnp.bfloat16)
    mixed = jnp.dot(hidden, w_down, preferred_element_type=jnp.float32)
    return (x + mixed + down_bias).astype(jnp.bfloat16)

def reference(handoff, ln_gain, ln_bias, w_up, up_bias, w_down, down_bias):
    first = section_block(handoff[1].astype(jnp.float32), ln_gain[0], ln_bias[0], w_up[0], up_bias[0], w_down[0], down_bias[0])
    second = section_block(handoff[0].astype(jnp.float32), ln_gain[1], ln_bias[1], w_up[1], up_bias[1], w_down[1], down_bias[1])
    return jnp.stack([first, second])
```

```python
import functools

import jax
import jax.numpy as jnp
from jax import lax
from jax.experimental import pallas as pl
from jax.experimental.pallas import tpu as pltpu
from jax.sharding import PartitionSpec as P

D = 12288
W = 1536
N = 8
CA = 768
CB = W - CA
HA = CA // 2
F32 = jnp.float32
BF16 = jnp.bfloat16
MESH = pl.DeviceIdType.MESH

OFFSETS = {"s2": 1, "s3": 2, "s4": 3, "s5": 4, "s6": 5, "g2": 6}
ORDER = ("ag", "g1", "s2", "s3", "s4", "s5", "s6", "g2", "z")
AG_SLOT = {1: 1, 2: 2, 3: 3, 4: 3}
Z_SLOT = {4: 9, 3: 11, 2: 13, 1: 14, 0: 14}
SLOTS = 15

SCRATCH = dict(
    hand=((8, D), BF16),
    wup=((W, W), BF16),
    wdn=((W, W), BF16),
    gain=((1, W), F32),
    bias=((1, W), F32),
    ubias=((1, W), F32),
    dbias=((1, W), F32),
    hs=((8, 16, 896), BF16),
    hr=((8, 16, 896), BF16),
    xres=((64, W), F32),
    nrm=((N, 128, W), BF16),
    paf=((N, 128, CA), F32),
    pbf=((N, 128, CB), F32),
    pab=((N, 128, CA), BF16),
    pbb=((N, 128, CB), BF16),
    a1=((N, 64, CA), BF16),
    a2=((N, 2, 16, HA), BF16),
    a3=((N, 2, 16, CA), BF16),
    b1=((N, 2, 16, CB), BF16),
    b2=((N, 2, 32, CB), BF16),
    b3=((N, 16, CB), BF16),
    fa=((N, 2, 16, HA), BF16),
    na=((N, 2, 16, CA), BF16),
    nb=((N, 2, 32, CB), BF16),
    xb=((N, 16, CB), BF16),
    hida=((N, 128, CA), BF16),
    hidb=((N, 128, CB), BF16),
    pf=((N, 128, W), F32),
    so=((N, 64, W), BF16),
    sib=((N, 64, W), BF16),
    zs=((N, 64, W), BF16),
    zr=((N, 64, W), BF16),
)
SENDS = ("hand", "agc", "agz", "a1", "a2", "a3", "b1", "b2", "b3", "a4", "a5", "a6", "b4", "b5", "b6", "so", "zr")
RECVS = ("agc", "agz", "a1", "a2", "a3", "b1", "b2", "b3", "a4", "a5", "a6", "b4", "b5", "b6", "so", "zr")


def kernel(hand_in, gain_in, bias_in, wup_in, ubias_in, wdn_in, dbias_in, out, *refs):
    v = dict(zip(SCRATCH, refs))
    local_sem, hand_sem, send_sem, recv_sem = refs[len(SCRATCH):]
    s = lax.axis_index("section")
    d = lax.axis_index("dp")
    m = lax.axis_index("mp")
    xl, y, z, c = d // 4, d % 4, m // 2, m % 2
    y_up, y_far, y_dn = (y + 1) % 4, (y + 2) % 4, (y + 3) % 4
    z_up, z_dn = (z + 1) % N, (z + N - 1) % N

    def at(section=s, x=xl, row=y, deep=z, core=c):
        return (section, x * 4 + row, deep * 2 + core)

    sibling = at(core=1 - c)
    x_other = at(x=1 - xl)
    above, below = at(row=y_up), at(row=y_dn)
    ahead, behind = at(deep=z_up), at(deep=z_dn)

    loads = []
    for i, (src, dst) in enumerate((
        (hand_in, "hand"), (gain_in, None), (bias_in, None), (ubias_in, None), (dbias_in, None),
        (wup_in, "wup"), (wdn_in, "wdn"),
    )):
        name = ("hand", "gain", "bias", "ubias", "dbias", "wup", "wdn")[i]
        from_ref = src.at[0] if dst else src
        load = pltpu.make_async_copy(from_ref, v[name], local_sem.at[i])
        load.start()
        loads.append(load)

    barrier = pltpu.get_barrier_semaphore()
    others = [(1 - s, i, m) for i in range(8)]
    near = [sibling, x_other, above, below, ahead, behind]
    for device in others + near:
        pl.semaphore_signal(barrier, inc=1, device_id=device, device_id_type=MESH)

    def send(kind, k, src, dst, device):
        pltpu.make_async_remote_copy(
            src_ref=src,
            dst_ref=dst,
            send_sem=send_sem.at[SENDS.index(kind)],
            recv_sem=recv_sem.at[RECVS.index(kind), k],
            device_id=device,
            device_id_type=MESH,
        ).start()

    def arrived(kind, k, like):
        pltpu.make_async_copy(like, like, recv_sem.at[RECVS.index(kind), k]).wait()

    def rows(start, size):
        return pl.ds(pl.multiple_of(start, 16), size)

    loads[0].wait()
    x = v["hand"][...].astype(F32)
    mean = jnp.sum(x, axis=1, keepdims=True) / D
    centred = x - mean
    rstd = lax.rsqrt(jnp.sum(centred * centred, axis=1, keepdims=True) / D + 1e-05)
    lane = lax.broadcasted_iota(jnp.int32, (8, 128), 1)

    def parts(value):
        high = value.astype(BF16).astype(F32)
        rest = value - high
        middle = rest.astype(BF16).astype(F32)
        low = rest - middle
        return jnp.where(lane < 32, high, jnp.where(lane < 64, middle, low))

    stats = jnp.concatenate([parts(mean), parts(rstd)], axis=0).astype(BF16)
    for i in range(8):
        left = x[:, i * W:i * W + 768]
        right = x[:, i * W + 768:(i + 1) * W]
        v["hs"][i, :, :768] = jnp.concatenate([left, right], axis=0).astype(BF16)
        v["hs"][i, :, 768:] = stats
    pl.semaphore_wait(barrier, len(others) + len(near))
    for i in range(8):
        pltpu.make_async_remote_copy(
            src_ref=v["hs"].at[i],
            dst_ref=v["hr"].at[d],
            send_sem=send_sem.at[0],
            recv_sem=hand_sem,
            device_id=others[i],
            device_id_type=MESH,
        ).start()
    for load in loads[1:5]:
        load.wait()
    pltpu.make_async_copy(v["hr"], v["hr"], hand_sem).wait()

    def unpack(i):
        held = v["hr"][i].astype(F32)
        stat = held[:, 768:]
        stat = stat[:, 0:1] + stat[:, 32:33] + stat[:, 64:65]
        return jnp.concatenate([held[:8, :768], held[8:, :768]], axis=1), stat[:8], stat[8:]

    for i in range(4):
        xa, mean_a, rstd_a = unpack(2 * i)
        xb, mean_b, rstd_b = unpack(2 * i + 1)
        two = jnp.concatenate([(xa - mean_a) * rstd_a, (xb - mean_b) * rstd_b], axis=0)
        v["nrm"][z, rows(c * 64 + i * 16, 16), :] = (two * v["gain"][...] + v["bias"][...]).astype(BF16)
        v["xres"][i * 16:i * 16 + 16, :] = jnp.concatenate([xa, xb], axis=0)

    def rel(k):
        return k + jnp.where(k == 3, 1, 0) - jnp.where(k == 4, 1, 0)

    def pos(r):
        return {4: 3, 3: 4}.get(r, r)

    def block(r, first=0, size=64):
        return v["nrm"].at[(z + r) % N, rows(c * 64 + first, size)]

    def ring(r, first, size, device, there):
        send("agz", there % N, block(r, first, size), block(r, first, size), device)

    def pair(r):
        send("agc", r % N, block(r), block(r), sibling)

    pair(0)
    ring(0, 0, 64, ahead, -1)
    ring(0, 0, 64, behind, 1)

    def gather(h):
        if h == 4:
            arrived("agz", 4, v["zr"].at[0])
            pair(4)
            return
        for r, device, step in ((-h, ahead, -1), (h, behind, 1)):
            arrived("agz", r % N, v["zr"].at[0])
            if h < 3:
                ring(r, 0, 64, device, r + step)
            else:
                ring(r, 0 if step < 0 else 32, 32, device, 4)
            pair(r)

    def g1(k):
        r = rel(k)
        own = (z + r) % N
        arrived("agc", r, v["zr"].at[0])
        for n in range(6):
            part = jnp.dot(v["nrm"][own], v["wup"][:, n * 256:n * 256 + 256], preferred_element_type=F32)
            first = n * 256
            f, b, first = ("paf", "pab", first) if first < CA else ("pbf", "pbb", first - CA)
            v[f][k, :, first:first + 256] = part
            v[b][k, :, first:first + 256] = part.astype(BF16)
        send("a1", k, v["pab"].at[k, rows((1 - xl) * 64, 64)], v["a1"].at[k], x_other)
        send("b1", k, v["pbb"].at[k, rows(y_far * 32, 16)], v["b1"].at[k, 0], above)
        send("b1", k, v["pbb"].at[k, rows(y_far * 32 + 16, 16)], v["b1"].at[k, 1], below)

    def s2(k):
        arrived("a1", k, v["a1"].at[k])
        mine = rows(xl * 64, 64)
        v["paf"][k, mine, :] = v["paf"][k, mine, :] + v["a1"][k].astype(F32)
        far = v["paf"][k, rows(xl * 64 + y_far * 16, 16), :].astype(BF16)
        v["fa"][k, 0] = far[:, :HA]
        v["fa"][k, 1] = far[:, HA:]
        send("a2", k, v["fa"].at[k, 0], v["a2"].at[k, 0], above)
        send("a2", k, v["fa"].at[k, 1], v["a2"].at[k, 1], below)
        arrived("b1", k, v["b1"].at[k])
        v["nb"][k, 0, :16] = (v["pbf"][k, rows(y_up * 32, 16), :] + v["b1"][k, 0].astype(F32)).astype(BF16)
        v["nb"][k, 0, 16:] = v["pbb"][k, rows(y_up * 32 + 16, 16), :]
        send("b2", k, v["nb"].at[k, 0], v["b2"].at[k, 0], above)
        v["nb"][k, 1, :16] = v["pbb"][k, rows(y_dn * 32, 16), :]
        v["nb"][k, 1, 16:] = (v["pbf"][k, rows(y_dn * 32 + 16, 16), :] + v["b1"][k, 1].astype(F32)).astype(BF16)
        send("b2", k, v["nb"].at[k, 1], v["b2"].at[k, 1], below)

    def s3(k):
        arrived("a2", k, v["a2"].at[k])
        up = v["paf"][k, rows(xl * 64 + y_up * 16, 16), :]
        v["na"][k, 0, :, :HA] = (up[:, :HA] + v["a2"][k, 0].astype(F32)).astype(BF16)
        v["na"][k, 0, :, HA:] = up[:, HA:].astype(BF16)
        send("a3", k, v["na"].at[k, 0], v["a3"].at[k, 0], above)
        down = v["paf"][k, rows(xl * 64 + y_dn * 16, 16), :]
        v["na"][k, 1, :, :HA] = down[:, :HA].astype(BF16)
        v["na"][k, 1, :, HA:] = (down[:, HA:] + v["a2"][k, 1].astype(F32)).astype(BF16)
        send("a3", k, v["na"].at[k, 1], v["a3"].at[k, 1], below)
        arrived("b2", k, v["b2"].at[k])
        mine = rows(y * 32, 32)
        v["pbf"][k, mine, :] = v["pbf"][k, mine, :] + v["b2"][k, 0].astype(F32) + v["b2"][k, 1].astype(F32)
        v["xb"][k] = v["pbf"][k, rows(y * 32 + (1 - xl) * 16, 16), :].astype(BF16)
        send("b3", k, v["xb"].at[k], v["b3"].at[k], x_other)

    def s4(k):
        arrived("a3", k, v["a3"].at[k])
        mine = rows(xl * 64 + y * 16, 16)
        total = v["paf"][k, mine, :] + v["a3"][k, 0].astype(F32) + v["a3"][k, 1].astype(F32)
        v["hida"][k, mine, :] = jnp.maximum(total + v["ubias"][:, :CA], 0.0).astype(BF16)
        here = v["hida"].at[k, mine]
        send("a4", k, here, here, above)
        send("a4", k, here, here, below)
        arrived("b3", k, v["b3"].at[k])
        mine = rows(y * 32 + xl * 16, 16)
        total = v["pbf"][k, mine, :] + v["b3"][k].astype(F32)
        v["hidb"][k, mine, :] = jnp.maximum(total + v["ubias"][:, CA:], 0.0).astype(BF16)
        here = v["hidb"].at[k, mine]
        send("b4", k, here, here, x_other)

    def s5(k):
        arrived("a4", k, v["a3"].at[k])
        here = v["hida"].at[k, rows(xl * 64 + y_dn * 16, 16), pl.ds(0, HA)]
        send("a5", k, here, here, above)
        here = v["hida"].at[k, rows(xl * 64 + y_up * 16, 16), pl.ds(HA, HA)]
        send("a5", k, here, here, below)
        arrived("b4", k, v["b3"].at[k])
        here = v["hidb"].at[k, rows(y * 32, 32)]
        send("b5", k, here, here, above)
        send("b5", k, here, here, below)

    def s6(k):
        arrived("a5", k, v["a2"].at[k])
        here = v["hida"].at[k, rows(xl * 64, 64)]
        send("a6", k, here, here, x_other)
        arrived("b5", k, v["b2"].at[k])
        here = v["hidb"].at[k, rows(y_dn * 32, 16)]
        send("b6", k, here, here, above)
        here = v["hidb"].at[k, rows(y_up * 32 + 16, 16)]
        send("b6", k, here, here, below)

    def g2(k):
        arrived("a6", k, v["a1"].at[k])
        arrived("b6", k, v["b1"].at[k])
        for n in range(6):
            cols = slice(n * 256, n * 256 + 256)
            v["pf"][k, :, cols] = jnp.dot(
                v["hida"][k], v["wdn"][:CA, cols], preferred_element_type=F32
            ) + jnp.dot(v["hidb"][k], v["wdn"][CA:, cols], preferred_element_type=F32)
        v["so"][k] = v["pf"][k, rows((1 - c) * 64, 64), :].astype(BF16)
        send("so", k, v["so"].at[k], v["sib"].at[k], sibling)

    def chip_sum(r, first=0, size=64):
        k = pos(r)
        return v["pf"][k, rows(c * 64 + first, size), :] + v["sib"][k, first:first + size].astype(F32)

    def scatter(h):
        if h == 4:
            arrived("so", pos(4), v["sib"].at[0])
            v["zs"][4] = chip_sum(4).astype(BF16)
            send("zr", 3, v["zs"].at[4, pl.ds(0, 32)], v["zr"].at[3, pl.ds(0, 32)], ahead)
            send("zr", 5, v["zs"].at[4, pl.ds(32, 32)], v["zr"].at[5, pl.ds(32, 32)], behind)
            return
        if h == 0:
            arrived("so", 0, v["sib"].at[0])
            arrived("zr", 0, v["zr"].at[0])
            arrived("zr", 4, v["zr"].at[4])
            total = v["xres"][...] + (chip_sum(0) + v["zr"][0].astype(F32) + v["zr"][4].astype(F32)) + v["dbias"][...]
            out[0] = total.astype(BF16)
            return
        for r, device, there in ((h, ahead, h - 1), (N - h, behind, (N - h + 1) % N or 4)):
            arrived("so", pos(r), v["sib"].at[0])
            if h == 3:
                first = 0 if r == 3 else 32
                arrived("zr", r, v["zr"].at[r, pl.ds(first, 32)])
                other = 32 - first
                v["zs"][r, first:first + 32] = (
                    chip_sum(r, first, 32) + v["zr"][r, first:first + 32].astype(F32)
                ).astype(BF16)
                v["zs"][r, other:other + 32] = chip_sum(r, other, 32).astype(BF16)
            else:
                arrived("zr", r, v["zr"].at[r])
                v["zs"][r] = (chip_sum(r) + v["zr"][r].astype(F32)).astype(BF16)
            send("zr", there, v["zs"].at[r], v["zr"].at[there], device)

    steps = dict(s2=s2, s3=s3, s4=s4, s5=s5, s6=s6, g2=g2)
    loads[5].wait()

    def slot(t, _):
        for name in ORDER:
            if name == "ag":
                for h, when in AG_SLOT.items():
                    pl.when(t == when)(functools.partial(gather, h))
            elif name == "z":
                for h, when in Z_SLOT.items():
                    pl.when(t == when)(functools.partial(scatter, h))
            elif name == "g1":
                pl.when(t < N)(functools.partial(g1, t))
            else:
                k = t - OFFSETS[name]
                pl.when((k >= 0) & (k < N))(functools.partial(steps[name], k))
        return 0

    loads[6].wait()
    lax.fori_loop(0, SLOTS, slot, 0)

    sent = dict(
        hand=v["hs"], agc=v["zr"], agz=v["zr"].at[pl.ds(0, 7)], a1=v["a1"], a2=v["a2"], a3=v["a3"],
        b1=v["b1"], b2=v["b2"], b3=v["b3"], a4=v["a3"], a5=v["a2"], a6=v["a1"], b4=v["b3"], b5=v["b2"],
        b6=v["b1"], so=v["sib"], zr=v["zr"].at[pl.ds(0, 7)],
    )
    for kind, like in sent.items():
        pltpu.make_async_copy(like, like, send_sem.at[SENDS.index(kind)]).wait()


def body(handoff, ln_gain, ln_bias, w_up, up_bias, w_down, down_bias):
    return pl.pallas_call(
        kernel,
        out_shape=jax.ShapeDtypeStruct((1, 64, W), BF16),
        in_specs=[pl.BlockSpec(memory_space=pl.ANY)] * 7,
        out_specs=pl.BlockSpec(memory_space=pltpu.VMEM),
        scratch_shapes=[pltpu.VMEM(shape, dtype) for shape, dtype in SCRATCH.values()] + [
            pltpu.SemaphoreType.DMA((7,)),
            pltpu.SemaphoreType.DMA,
            pltpu.SemaphoreType.DMA((len(SENDS),)),
            pltpu.SemaphoreType.DMA((len(RECVS), N)),
        ],
        compiler_params=pltpu.CompilerParams(
            collective_id=0, has_side_effects=True, vmem_limit_bytes=60 << 20
        ),
        name="relay_block",
    )(handoff, ln_gain, ln_bias, w_up, up_bias, w_down, down_bias)


def solution(mesh):
    placed = (
        P("section", ("mp", "dp"), None),
        P("section", "dp"),
        P("section", "dp"),
        P("section", "dp", "mp"),
        P("section", "mp"),
        P("section", "mp", "dp"),
        P("section", "dp"),
    )
    return jax.shard_map(
        body, mesh=mesh, in_specs=placed, out_specs=P("section", "mp", "dp"), check_vma=False
    )
```

```python
import jax
import jax.numpy as jnp
from jax import lax
from jax.experimental import pallas as pl
from jax.experimental.pallas import tpu as pltpu
from jax.sharding import PartitionSpec as P

D = 12288
W = 1536
N = 8
CA = 896
CB = W - CA
F32 = jnp.float32
BF16 = jnp.bfloat16
MESH = pl.DeviceIdType.MESH

ORDER = (
    ("ga", 1, 0), ("ga", 7, 0), ("g1", 0, 0), ("ga", 7, 1), ("ga", 1, 1), ("g1", 7, 0), ("ga", 6, 0), ("ga", 2, 0),
    ("g1", 1, 0), ("s2a", 0, 0), ("ga", 6, 1), ("ga", 2, 1), ("g1", 6, 0), ("g1", 2, 0), ("ga", 5, 0), ("s2a", 7, 0),
    ("ga", 3, 0), ("ga", 3, 1), ("ga", 5, 1), ("g1", 3, 0), ("s2a", 1, 0), ("g1", 5, 0), ("ga", 4, 0), ("ga", 4, 1),
    ("g1", 4, 0), ("s2b", 3, 0), ("s2a", 2, 0), ("s2b", 6, 0), ("s2a", 3, 0), ("s2b", 2, 0), ("s2b", 5, 0),
    ("s2b", 0, 0), ("s2a", 6, 0), ("s2b", 4, 0), ("s2b", 7, 0), ("s2a", 4, 0), ("s2b", 1, 0), ("s2a", 5, 0),
    ("s4b", 6, 0), ("s4b", 3, 0), ("s4b", 2, 0), ("s4b", 0, 0), ("s4a", 3, 0), ("s4b", 4, 0), ("s4a", 2, 0),
    ("s4b", 5, 0), ("s4a", 4, 0), ("s4b", 7, 0), ("s4a", 5, 0), ("s6b", 4, 0), ("s4a", 6, 0), ("s6b", 3, 0),
    ("s6a", 3, 0), ("s6b", 5, 0), ("s6b", 6, 0), ("s4a", 7, 0), ("s4a", 1, 0), ("s6a", 4, 0), ("s4b", 1, 0),
    ("s6a", 5, 0), ("s6a", 6, 0), ("s6b", 2, 0), ("s6a", 2, 0), ("g2", 4, 0), ("g2", 3, 0), ("z4", 4, 0),
    ("g2", 5, 0), ("s4a", 0, 0), ("s6b", 7, 0), ("s6a", 7, 0), ("z", 3, 1), ("s6b", 1, 0), ("z", 5, 0), ("g2", 6, 0),
    ("z", 3, 0), ("s6a", 1, 0), ("z", 5, 1), ("g2", 2, 0), ("z", 6, 0), ("s6a", 0, 0), ("s6b", 0, 0), ("z", 2, 1),
    ("g2", 7, 0), ("z", 6, 1), ("z", 2, 0), ("g2", 1, 0), ("z", 7, 0), ("z", 1, 1), ("z", 7, 1), ("z", 1, 0),
    ("g2", 0, 0), ("z", 0, 1), ("z", 0, 0),
)

SCRATCH = dict(
    hand=((8, D), BF16),
    wup=((W, W), BF16),
    wdn=((W, W), BF16),
    gain=((1, W), F32),
    bias=((1, W), F32),
    ubias=((1, W), F32),
    dbias=((1, W), F32),
    hs=((8, 16, 896), BF16),
    hr=((8, 16, 896), BF16),
    xres=((64, W), F32),
    nrm=((N, 128, W), BF16),
    paf=((N, 128, CA), F32),
    pbf=((N, 128, CB), F32),
    pab=((N, 128, CA), BF16),
    pbb=((N, 128, CB), BF16),
    a1=((N, 64, CA), BF16),
    a2=((N, 3, 16, CA), BF16),
    b1=((N, 3, 32, CB), BF16),
    b2=((N, 16, CB), BF16),
    sa=((N, 64, CA), BF16),
    sb=((N, 16, CB), BF16),
    hid=((N, 128, W), BF16),
    pf=((N, 128, W), F32),
    so=((N, 64, W), BF16),
    sib=((N, 64, W), BF16),
    zs=((N, 64, W), BF16),
    zr=((N, 64, W), BF16),
)
SENDS = ("hand", "agc", "agz", "a1", "b1", "a2", "b2", "a3", "b3", "a4", "b4", "so", "zr")
RECVS = ("agc", "agz", "a1", "b1", "a2", "b2", "a3", "b3", "a4", "b4", "so", "zr")


def kernel(hand_in, gain_in, bias_in, wup_in, ubias_in, wdn_in, dbias_in, out, *refs):
    v = dict(zip(SCRATCH, refs))
    local_sem, hand_sem, send_sem, recv_sem = refs[len(SCRATCH):]
    s = lax.axis_index("section")
    d = lax.axis_index("dp")
    m = lax.axis_index("mp")
    xl, y, z, c = d // 4, d % 4, m // 2, m % 2
    other_y = [(y + j) % 4 for j in (1, 2, 3)]
    z_up, z_dn = (z + 1) % N, (z + N - 1) % N

    def at(section=s, x=xl, row=y, deep=z, core=c):
        return (section, x * 4 + row, deep * 2 + core)

    sibling = at(core=1 - c)
    x_other = at(x=1 - xl)
    in_row = [at(row=row) for row in other_y]
    ahead, behind = at(deep=z_up), at(deep=z_dn)

    loads = []
    for i, (src, dst) in enumerate((
        (hand_in, "hand"), (gain_in, None), (bias_in, None), (ubias_in, None), (dbias_in, None),
        (wup_in, "wup"), (wdn_in, "wdn"),
    )):
        name = ("hand", "gain", "bias", "ubias", "dbias", "wup", "wdn")[i]
        from_ref = src.at[0] if dst else src
        load = pltpu.make_async_copy(from_ref, v[name], local_sem.at[i])
        load.start()
        loads.append(load)

    barrier = pltpu.get_barrier_semaphore()
    others = [(1 - s, i, m) for i in range(8)]
    near = [sibling, x_other, *in_row, ahead, behind]
    for device in others + near:
        pl.semaphore_signal(barrier, inc=1, device_id=device, device_id_type=MESH)

    def send(kind, k, src, dst, device):
        pltpu.make_async_remote_copy(
            src_ref=src,
            dst_ref=dst,
            send_sem=send_sem.at[SENDS.index(kind)],
            recv_sem=recv_sem.at[RECVS.index(kind), k],
            device_id=device,
            device_id_type=MESH,
        ).start()

    def arrived(kind, k, like):
        pltpu.make_async_copy(like, like, recv_sem.at[RECVS.index(kind), k]).wait()

    def rows(start, size):
        return pl.ds(pl.multiple_of(start, 16), size)

    loads[0].wait()
    x = v["hand"][...].astype(F32)
    mean = jnp.sum(x, axis=1, keepdims=True) / D
    centred = x - mean
    rstd = lax.rsqrt(jnp.sum(centred * centred, axis=1, keepdims=True) / D + 1e-05)
    lane = lax.broadcasted_iota(jnp.int32, (8, 128), 1)

    def parts(value):
        high = value.astype(BF16).astype(F32)
        rest = value - high
        middle = rest.astype(BF16).astype(F32)
        low = rest - middle
        return jnp.where(lane < 32, high, jnp.where(lane < 64, middle, low))

    stats = jnp.concatenate([parts(mean), parts(rstd)], axis=0).astype(BF16)
    for i in range(8):
        left = x[:, i * W:i * W + 768]
        right = x[:, i * W + 768:(i + 1) * W]
        v["hs"][i, :, :768] = jnp.concatenate([left, right], axis=0).astype(BF16)
        v["hs"][i, :, 768:] = stats
    pl.semaphore_wait(barrier, len(others) + len(near))
    for i in range(8):
        pltpu.make_async_remote_copy(
            src_ref=v["hs"].at[i],
            dst_ref=v["hr"].at[d],
            send_sem=send_sem.at[0],
            recv_sem=hand_sem,
            device_id=others[i],
            device_id_type=MESH,
        ).start()
    for load in loads[1:5]:
        load.wait()
    pltpu.make_async_copy(v["hr"], v["hr"], hand_sem).wait()

    def unpack(i):
        held = v["hr"][i].astype(F32)
        stat = held[:, 768:]
        stat = stat[:, 0:1] + stat[:, 32:33] + stat[:, 64:65]
        return jnp.concatenate([held[:8, :768], held[8:, :768]], axis=1), stat[:8], stat[8:]

    def block(r, h):
        return v["nrm"].at[(z + r) % N, rows(c * 64 + h * 32, 32)]

    def pair(r, h):
        send("agc", r % N, block(r, h), block(r, h), sibling)

    def ring(r, h, step):
        send("agz", (r + step) % N * 2 + h, block(r, h), block(r, h), ahead if step < 0 else behind)

    for i in range(4):
        xa, mean_a, rstd_a = unpack(2 * i)
        xb, mean_b, rstd_b = unpack(2 * i + 1)
        two = jnp.concatenate([(xa - mean_a) * rstd_a, (xb - mean_b) * rstd_b], axis=0)
        v["nrm"][z, rows(c * 64 + i * 16, 16), :] = (two * v["gain"][...] + v["bias"][...]).astype(BF16)
        v["xres"][i * 16:i * 16 + 16, :] = jnp.concatenate([xa, xb], axis=0)
        if i % 2:
            ring(0, i // 2, -1)
            ring(0, i // 2, 1)
            pair(0, i // 2)

    def ga(r, h):
        arrived("agz", r * 2 + h, v["zr"].at[0, pl.ds(0, 32)])
        step = -1 if r > 4 else 1
        if r != 4 and (r + step != 4 or h == (0 if step < 0 else 1)):
            ring(r, h, step)
        pair(r, h)

    def g1(r):
        own = (z + r) % N
        arrived("agc", r, v["zr"].at[0])
        for n in range(0, W, 256):
            part = jnp.dot(v["nrm"][own], v["wup"][:, n:n + 256], preferred_element_type=F32)
            low = min(max(CA - n, 0), 256)
            if low:
                v["paf"][r, :, n:n + low] = part[:, :low]
                v["pab"][r, :, n:n + low] = part[:, :low].astype(BF16)
            if low < 256:
                v["pbf"][r, :, n + low - CA:n + 256 - CA] = part[:, low:]
                v["pbb"][r, :, n + low - CA:n + 256 - CA] = part[:, low:].astype(BF16)
        send("a1", r, v["pab"].at[r, rows((1 - xl) * 64, 64)], v["a1"].at[r], x_other)
        for j in (0, 2, 1):
            send("b1", r, v["pbb"].at[r, rows(other_y[j] * 32, 32)], v["b1"].at[r, j], in_row[j])

    def s2a(r):
        arrived("a1", r, v["a1"].at[r])
        total = v["paf"][r, rows(xl * 64, 64), :] + v["a1"][r].astype(F32)
        v["paf"][r, rows(xl * 64, 64), :] = total
        v["sa"][r] = total.astype(BF16)
        for j in (0, 2, 1):
            send("a2", r, v["sa"].at[r, rows(other_y[j] * 16, 16)], v["a2"].at[r, j], in_row[j])

    def s2b(r):
        arrived("b1", r, v["b1"].at[r])

        def total(x):
            sums = v["pbf"][r, rows(y * 32 + x * 16, 16), :]
            for j in range(3):
                sums = sums + v["b1"][r, j, rows(x * 16, 16), :].astype(F32)
            return sums

        v["sb"][r] = total(1 - xl).astype(BF16)
        send("b2", r, v["sb"].at[r], v["b2"].at[r], x_other)
        v["pbf"][r, rows(y * 32 + xl * 16, 16), :] = total(xl)

    def s4a(r):
        arrived("a2", r, v["a2"].at[r])
        mine = rows(xl * 64 + y * 16, 16)
        total = v["paf"][r, mine, :]
        for j in range(3):
            total = total + v["a2"][r, j].astype(F32)
        v["hid"][r, mine, :CA] = jnp.maximum(total + v["ubias"][:, :CA], 0.0).astype(BF16)
        here = v["hid"].at[r, mine, pl.ds(0, CA)]
        for j in (0, 2, 1):
            send("a3", r, here, here, in_row[j])

    def s4b(r):
        arrived("b2", r, v["b2"].at[r])
        mine = rows(y * 32 + xl * 16, 16)
        total = v["pbf"][r, mine, :] + v["b2"][r].astype(F32)
        v["hid"][r, mine, CA:] = jnp.maximum(total + v["ubias"][:, CA:], 0.0).astype(BF16)
        here = v["hid"].at[r, mine, pl.ds(CA, CB)]
        send("b3", r, here, here, x_other)

    def s6a(r):
        arrived("a3", r, v["a2"].at[r])
        here = v["hid"].at[r, rows(xl * 64, 64), pl.ds(0, CA)]
        send("a4", r, here, here, x_other)

    def s6b(r):
        arrived("b3", r, v["b2"].at[r])
        here = v["hid"].at[r, rows(y * 32, 32), pl.ds(CA, CB)]
        for j in (0, 2, 1):
            send("b4", r, here, here, in_row[j])

    def g2(r):
        arrived("a4", r, v["a1"].at[r])
        arrived("b4", r, v["b1"].at[r])
        for n in range(0, W, 256):
            v["pf"][r, :, n:n + 256] = jnp.dot(v["hid"][r], v["wdn"][:, n:n + 256], preferred_element_type=F32)
        v["so"][r] = v["pf"][r, rows((1 - c) * 64, 64), :].astype(BF16)
        send("so", r, v["so"].at[r], v["sib"].at[r], sibling)

    def chip_sum(r, h):
        return v["pf"][r, rows(c * 64 + h * 32, 32), :] + v["sib"][r, h * 32:h * 32 + 32].astype(F32)

    summed = set()

    def z_sum(r, h):
        if r not in summed:
            arrived("so", r, v["sib"].at[r])
            summed.add(r)
        half = pl.ds(h * 32, 32)
        total = chip_sum(r, h)
        if r in (1, 2, 6, 7) or (r, h) in ((3, 0), (5, 1)):
            arrived("zr", r * 2 + h, v["zr"].at[r, half])
            total = total + v["zr"][r, half].astype(F32)
        v["zs"][r, half] = total.astype(BF16)
        step = -1 if r < 4 or (r == 4 and h == 0) else 1
        there = (r + step) % N
        there = 4 if there == 0 and step > 0 else there
        send("zr", there * 2 + h, v["zs"].at[r, half], v["zr"].at[there, half], ahead if step < 0 else behind)

    def finish(h):
        if 0 not in summed:
            arrived("so", 0, v["sib"].at[0])
            summed.add(0)
        half = pl.ds(h * 32, 32)
        arrived("zr", h, v["zr"].at[0, half])
        arrived("zr", 8 + h, v["zr"].at[4, half])
        mixed = chip_sum(0, h) + v["zr"][0, half].astype(F32) + v["zr"][4, half].astype(F32)
        out[0, h * 32:h * 32 + 32] = (v["xres"][h * 32:h * 32 + 32] + mixed + v["dbias"][...]).astype(BF16)

    loads[5].wait()
    first_down = True
    chunk_steps = dict(g1=g1, s2a=s2a, s2b=s2b, s4a=s4a, s4b=s4b, s6a=s6a, s6b=s6b, g2=g2)
    for name, r, h in ORDER:
        if name == "g2" and first_down:
            loads[6].wait()
            first_down = False
        if name == "ga":
            ga(r, h)
        elif name == "z4":
            z_sum(4, 0)
            z_sum(4, 1)
        elif name == "z" and r == 0:
            finish(h)
        elif name == "z":
            z_sum(r, h)
        else:
            chunk_steps[name](r)

    sent = dict(
        hand=v["hs"], agc=v["zr"], agz=v["zr"].at[pl.ds(0, 7)], a1=v["a1"], b1=v["b1"], a2=v["a2"], b2=v["b2"],
        a3=v["a2"], b3=v["b2"], a4=v["a1"], b4=v["b1"], so=v["sib"], zr=v["zr"].at[pl.ds(0, 7)],
    )
    for kind, like in sent.items():
        pltpu.make_async_copy(like, like, send_sem.at[SENDS.index(kind)]).wait()


def body(handoff, ln_gain, ln_bias, w_up, up_bias, w_down, down_bias):
    return pl.pallas_call(
        kernel,
        out_shape=jax.ShapeDtypeStruct((1, 64, W), BF16),
        in_specs=[pl.BlockSpec(memory_space=pl.ANY)] * 7,
        out_specs=pl.BlockSpec(memory_space=pltpu.VMEM),
        scratch_shapes=[pltpu.VMEM(shape, dtype) for shape, dtype in SCRATCH.values()] + [
            pltpu.SemaphoreType.DMA((7,)),
            pltpu.SemaphoreType.DMA,
            pltpu.SemaphoreType.DMA((len(SENDS),)),
            pltpu.SemaphoreType.DMA((len(RECVS), 2 * N)),
        ],
        compiler_params=pltpu.CompilerParams(
            collective_id=0, has_side_effects=True, vmem_limit_bytes=60 << 20
        ),
        name="relay_block",
    )(handoff, ln_gain, ln_bias, w_up, up_bias, w_down, down_bias)


def solution(mesh):
    placed = (
        P("section", ("mp", "dp"), None),
        P("section", "dp"),
        P("section", "dp"),
        P("section", "dp", "mp"),
        P("section", "mp"),
        P("section", "mp", "dp"),
        P("section", "dp"),
    )
    return jax.shard_map(
        body, mesh=mesh, in_specs=placed, out_specs=P("section", "mp", "dp"), check_vma=False
    )
```

```python
import jax
import jax.numpy as jnp
from jax import lax
from jax.experimental import pallas as pl
from jax.experimental.pallas import tpu as pltpu
from jax.sharding import PartitionSpec as P

D = 12288
W = 1536
N = 8
CA = 768
CB = W - CA
HA = CA // 2
CUTS = 4
PIECE = 64 // CUTS
DIRECT = ()
F32 = jnp.float32
BF16 = jnp.bfloat16
MESH = pl.DeviceIdType.MESH

ORDER = (
    ("n", 0, 0), ("n", 0, 1), ("n", 0, 2), ("n", 0, 3), ("ga", 1, 0), ("ga", 7, 0), ("ga", 1, 1), ("ga", 7, 1),
    ("g1", 0, 0), ("ga", 1, 2), ("ga", 7, 2), ("ga", 7, 3), ("ga", 1, 3), ("ga", 6, 0), ("ga", 2, 0), ("g1", 7, 0),
    ("ga", 2, 1), ("g1", 1, 0), ("ga", 6, 1), ("s2a", 0, 0), ("ga", 2, 2), ("s2b", 0, 0), ("ga", 2, 3), ("ga", 6, 2),
    ("ga", 6, 3), ("ga", 5, 0), ("s2b", 7, 0), ("g1", 2, 0), ("g1", 6, 0), ("ga", 3, 2), ("s2a", 7, 0), ("ga", 3, 1),
    ("ga", 5, 1), ("s2b", 1, 0), ("ga", 3, 0), ("ga", 3, 3), ("s2a", 1, 0), ("ga", 5, 3), ("ga", 5, 2), ("s3a", 0, 0),
    ("s2b", 2, 0), ("g1", 3, 0), ("ga", 4, 0), ("g1", 5, 0), ("ga", 4, 2), ("s2b", 6, 0), ("s2a", 2, 0),
    ("s3a", 7, 0), ("ga", 4, 1), ("ga", 4, 3), ("g1", 4, 0), ("s2b", 3, 0), ("s3b", 0, 0), ("s2a", 3, 0),
    ("s3a", 1, 0), ("s2a", 6, 0), ("s3a", 2, 0), ("s3b", 7, 0), ("s2b", 4, 0), ("s3b", 2, 0), ("s3b", 1, 0),
    ("s3b", 3, 0), ("s3a", 3, 0), ("s2a", 4, 0), ("s2b", 5, 0), ("s2a", 5, 0), ("s4a", 1, 0), ("s4b", 7, 0),
    ("s3b", 4, 0), ("s4b", 1, 0), ("s4a", 3, 0), ("s4b", 0, 0), ("s4b", 3, 0), ("s3a", 4, 0), ("s4a", 7, 0),
    ("s3a", 6, 0), ("s3b", 5, 0), ("s3a", 5, 0), ("s4a", 2, 0), ("s4b", 4, 0), ("s4b", 2, 0), ("s5a", 3, 0),
    ("s3b", 6, 0), ("s4a", 4, 0), ("s5b", 3, 0), ("s4a", 5, 0), ("s5b", 4, 0), ("s4b", 5, 0), ("s4b", 6, 0),
    ("s5a", 4, 0), ("s4a", 6, 0), ("s6a", 3, 0), ("s6b", 3, 0), ("s5a", 5, 0), ("s5b", 5, 0), ("s6b", 4, 0),
    ("s5a", 2, 0), ("s6a", 4, 0), ("s5a", 7, 0), ("s5b", 2, 0), ("s5a", 6, 0), ("s5b", 6, 0), ("s6a", 5, 0),
    ("s5a", 1, 0), ("g2", 3, 0), ("s6b", 5, 0), ("s6a", 2, 0), ("g2", 4, 0), ("z", 3, 2), ("s5b", 1, 0),
    ("s6a", 6, 0), ("s6b", 2, 0), ("s5b", 7, 0), ("s6a", 1, 0), ("z", 4, 0), ("z", 4, 2), ("g2", 5, 0), ("s6b", 6, 0),
    ("z", 4, 3), ("z", 4, 1), ("s4a", 0, 0), ("z", 3, 3), ("z", 5, 0), ("z", 5, 1), ("g2", 2, 0), ("s6a", 7, 0),
    ("z", 3, 0), ("z", 5, 2), ("s6b", 1, 0), ("s6b", 7, 0), ("s5b", 0, 0), ("g2", 6, 0), ("z", 5, 3), ("z", 3, 1),
    ("s5a", 0, 0), ("z", 2, 2), ("z", 6, 0), ("z", 2, 3), ("g2", 1, 0), ("z", 6, 1), ("z", 6, 2), ("z", 2, 0),
    ("g2", 7, 0), ("z", 6, 3), ("z", 2, 1), ("z", 1, 2), ("s6a", 0, 0), ("s6b", 0, 0), ("z", 7, 0), ("z", 1, 3),
    ("z", 7, 1), ("z", 7, 2), ("z", 1, 0), ("z", 7, 3), ("z", 1, 1), ("g2", 0, 0), ("z", 0, 1), ("z", 0, 0),
    ("z", 0, 2), ("z", 0, 3),
)

SCRATCH = dict(
    hand=((8, D), BF16),
    wup=((W, W), BF16),
    wdn=((W, W), BF16),
    gain=((1, W), F32),
    bias=((1, W), F32),
    ubias=((1, W), F32),
    dbias=((1, W), F32),
    hs=((8, 16, 896), BF16),
    hr=((8, 16, 896), BF16),
    xres=((64, W), F32),
    nrm=((N, 128, W), BF16),
    paf=((N, 128, CA), F32),
    pbf=((N, 128, CB), F32),
    pab=((N, 128, CA), BF16),
    pbb=((N, 128, CB), BF16),
    a1=((N, 64, CA), BF16),
    a2=((N, 2, 16, HA), BF16),
    a3=((N, 2, 16, CA), BF16),
    a2d=((N, 3, 16, CA), BF16),
    b1=((N, 2, 16, CB), BF16),
    b2=((N, 2, 32, CB), BF16),
    b1d=((N, 3, 32, CB), BF16),
    b3=((N, 16, CB), BF16),
    sa=((N, 64, CA), BF16),
    sa2=((N, 2, 16, CA), BF16),
    sb2=((N, 2, 32, CB), BF16),
    sb=((N, 16, CB), BF16),
    hid=((N, 128, W), BF16),
    pf=((N, 128, W), F32),
    so=((N, 64, W), BF16),
    sib=((N, 64, W), BF16),
    zs=((N, 64, W), BF16),
    zr=((N, 64, W), BF16),
)
KINDS = (
    "agc", "agz", "a1", "a2", "a3", "a2d", "b1", "b2", "b1d", "b3",
    "a4", "a5", "a3d", "a6", "b4", "b5", "b6", "b4d", "so", "zr",
)
SENDS = ("hand",) + KINDS
LANDINGS = 168


def kernel(hand_in, gain_in, bias_in, wup_in, ubias_in, wdn_in, dbias_in, out, *refs):
    v = dict(zip(SCRATCH, refs))
    local_sem, hand_sem, send_sem, recv_sem = refs[len(SCRATCH):]
    s = lax.axis_index("section")
    d = lax.axis_index("dp")
    m = lax.axis_index("mp")
    xl, y, z, c = d // 4, d % 4, m // 2, m % 2
    other_y = [(y + j) % 4 for j in (1, 2, 3)]
    z_up, z_dn = (z + 1) % N, (z + N - 1) % N

    def at(section=s, x=xl, row=y, deep=z, core=c):
        return (section, x * 4 + row, deep * 2 + core)

    sibling = at(core=1 - c)
    x_other = at(x=1 - xl)
    in_row = [at(row=row) for row in other_y]
    y_up, y_far, y_dn = other_y
    above, below = in_row[0], in_row[2]
    ahead, behind = at(deep=z_up), at(deep=z_dn)

    loads = []
    for i, (src, dst) in enumerate((
        (hand_in, "hand"), (gain_in, None), (bias_in, None), (ubias_in, None), (dbias_in, None),
        (wup_in, "wup"), (wdn_in, "wdn"),
    )):
        name = ("hand", "gain", "bias", "ubias", "dbias", "wup", "wdn")[i]
        from_ref = src.at[0] if dst else src
        load = pltpu.make_async_copy(from_ref, v[name], local_sem.at[i])
        load.start()
        loads.append(load)

    barrier = pltpu.get_barrier_semaphore()
    others = [(1 - s, i, m) for i in range(8)]
    near = [sibling, x_other, *in_row, ahead, behind]
    for device in others + near:
        pl.semaphore_signal(barrier, inc=1, device_id=device, device_id_type=MESH)

    slots = {}

    def landed(kind, k):
        return recv_sem.at[slots.setdefault((kind, k), len(slots))]

    def send(kind, k, src, dst, device):
        pltpu.make_async_remote_copy(
            src_ref=src,
            dst_ref=dst,
            send_sem=send_sem.at[SENDS.index(kind)],
            recv_sem=landed(kind, k),
            device_id=device,
            device_id_type=MESH,
        ).start()

    def arrived(kind, k, like):
        pltpu.make_async_copy(like, like, landed(kind, k)).wait()

    def rows(start, size):
        return pl.ds(pl.multiple_of(start, 16), size)

    loads[0].wait()
    x = v["hand"][...].astype(F32)
    mean = jnp.sum(x, axis=1, keepdims=True) / D
    centred = x - mean
    rstd = lax.rsqrt(jnp.sum(centred * centred, axis=1, keepdims=True) / D + 1e-05)
    lane = lax.broadcasted_iota(jnp.int32, (8, 128), 1)

    def parts(value):
        high = value.astype(BF16).astype(F32)
        rest = value - high
        middle = rest.astype(BF16).astype(F32)
        low = rest - middle
        return jnp.where(lane < 32, high, jnp.where(lane < 64, middle, low))

    stats = jnp.concatenate([parts(mean), parts(rstd)], axis=0).astype(BF16)
    for i in range(8):
        left = x[:, i * W:i * W + 768]
        right = x[:, i * W + 768:(i + 1) * W]
        v["hs"][i, :, :768] = jnp.concatenate([left, right], axis=0).astype(BF16)
        v["hs"][i, :, 768:] = stats
    pl.semaphore_wait(barrier, len(others) + len(near))
    def partner(step):
        low = 1 - d % 2 if step % 2 else d % 2
        return (d // 2 + step // 2) % 4 * 2 + low

    for i in range(8):
        other = partner(i)
        pltpu.make_async_remote_copy(
            src_ref=v["hs"].at[other],
            dst_ref=v["hr"].at[d],
            send_sem=send_sem.at[0],
            recv_sem=hand_sem.at[i // 2],
            device_id=(1 - s, other, m),
            device_id_type=MESH,
        ).start()
    for load in loads[1:5]:
        load.wait()

    def piece(p):
        return (d // 2 + 4 - p) % 4 * 16

    def unpack(i):
        held = v["hr"][i].astype(F32)
        stat = held[:, 768:]
        stat = stat[:, 0:1] + stat[:, 32:33] + stat[:, 64:65]
        return jnp.concatenate([held[:8, :768], held[8:, :768]], axis=1), stat[:8], stat[8:]

    def block(r, p):
        return v["nrm"].at[(z + r) % N, rows(c * 64 + piece(p), 16)]

    def pair(r, p):
        send("agc", r % N, block(r, p), block(r, p), sibling)

    def ring(r, h, step):
        send("agz", (r + step) % N * CUTS + h, block(r, h), block(r, h), ahead if step < 0 else behind)

    def normalize(p):
        pltpu.make_async_copy(v["hr"].at[pl.ds(0, 2)], v["hr"].at[pl.ds(0, 2)], hand_sem.at[p]).wait()
        first = piece(p) // 8
        xa, mean_a, rstd_a = unpack(first)
        xb, mean_b, rstd_b = unpack(first + 1)
        two = jnp.concatenate([(xa - mean_a) * rstd_a, (xb - mean_b) * rstd_b], axis=0)
        v["nrm"][z, rows(c * 64 + piece(p), 16), :] = (two * v["gain"][...] + v["bias"][...]).astype(BF16)
        v["xres"][rows(piece(p), 16), :] = jnp.concatenate([xa, xb], axis=0)
        ring(0, p, -1)
        ring(0, p, 1)
        pair(0, p)

    def ga(r, h):
        arrived("agz", r * CUTS + h, v["zr"].at[0, pl.ds(0, PIECE)])
        step = -1 if r > 4 else 1
        if r != 4 and (r + step != 4 or (h < CUTS // 2) == (step < 0)):
            ring(r, h, step)
        pair(r, h)

    def g1(r):
        own = (z + r) % N
        arrived("agc", r, v["zr"].at[0])
        for n in range(0, W, 256):
            part = jnp.dot(v["nrm"][own], v["wup"][:, n:n + 256], preferred_element_type=F32)
            f, b, first = ("paf", "pab", n) if n < CA else ("pbf", "pbb", n - CA)
            v[f][r, :, first:first + 256] = part
            v[b][r, :, first:first + 256] = part.astype(BF16)
        send("a1", r, v["pab"].at[r, rows((1 - xl) * 64, 64)], v["a1"].at[r], x_other)
        if r in DIRECT:
            for j in (0, 2, 1):
                send("b1d", r, v["pbb"].at[r, rows(other_y[j] * 32, 32)], v["b1d"].at[r, j], in_row[j])
        else:
            send("b1", r, v["pbb"].at[r, rows(y_far * 32, 16)], v["b1"].at[r, 0], above)
            send("b1", r, v["pbb"].at[r, rows(y_far * 32 + 16, 16)], v["b1"].at[r, 1], below)

    def s2a(r):
        arrived("a1", r, v["a1"].at[r])
        total = v["paf"][r, rows(xl * 64, 64), :] + v["a1"][r].astype(F32)
        v["paf"][r, rows(xl * 64, 64), :] = total
        v["sa"][r] = total.astype(BF16)
        if r in DIRECT:
            for j in (0, 2, 1):
                send("a2d", r, v["sa"].at[r, rows(other_y[j] * 16, 16)], v["a2d"].at[r, j], in_row[j])
        else:
            far = rows(y_far * 16, 16)
            send("a2", r, v["sa"].at[r, far, pl.ds(0, HA)], v["a2"].at[r, 0], above)
            send("a2", r, v["sa"].at[r, far, pl.ds(HA, HA)], v["a2"].at[r, 1], below)

    def x_sums(r, kind):
        def total(x):
            sums = v["pbf"][r, rows(y * 32 + x * 16, 16), :]
            for j in range(3 if kind == "b1d" else 2):
                sums = sums + v[kind][r, j, rows(x * 16, 16), :].astype(F32)
            return sums

        v["sb"][r] = total(1 - xl).astype(BF16)
        send("b3", r, v["sb"].at[r], v["b3"].at[r], x_other)
        v["pbf"][r, rows(y * 32 + xl * 16, 16), :] = total(xl)

    def s2b(r):
        if r in DIRECT:
            arrived("b1d", r, v["b1d"].at[r])
            x_sums(r, "b1d")
            return
        arrived("b1", r, v["b1"].at[r])
        up, down = rows(y_up * 32, 16), rows(y_dn * 32 + 16, 16)
        v["sb2"][r, 0, :16] = (v["pbf"][r, up, :] + v["b1"][r, 0].astype(F32)).astype(BF16)
        v["sb2"][r, 0, 16:] = v["pbb"][r, rows(y_up * 32 + 16, 16), :]
        send("b2", r, v["sb2"].at[r, 0], v["b2"].at[r, 0], above)
        v["sb2"][r, 1, :16] = v["pbb"][r, rows(y_dn * 32, 16), :]
        v["sb2"][r, 1, 16:] = (v["pbf"][r, down, :] + v["b1"][r, 1].astype(F32)).astype(BF16)
        send("b2", r, v["sb2"].at[r, 1], v["b2"].at[r, 1], below)

    def s3a(r):
        arrived("a2", r, v["a2"].at[r])
        up = v["paf"][r, rows(xl * 64 + y_up * 16, 16), :]
        v["sa2"][r, 0, :, :HA] = (up[:, :HA] + v["a2"][r, 0].astype(F32)).astype(BF16)
        v["sa2"][r, 0, :, HA:] = up[:, HA:].astype(BF16)
        send("a3", r, v["sa2"].at[r, 0], v["a3"].at[r, 0], above)
        down = v["paf"][r, rows(xl * 64 + y_dn * 16, 16), :]
        v["sa2"][r, 1, :, :HA] = down[:, :HA].astype(BF16)
        v["sa2"][r, 1, :, HA:] = (down[:, HA:] + v["a2"][r, 1].astype(F32)).astype(BF16)
        send("a3", r, v["sa2"].at[r, 1], v["a3"].at[r, 1], below)

    def s3b(r):
        arrived("b2", r, v["b2"].at[r])
        x_sums(r, "b2")

    def s4a(r):
        kind = "a2d" if r in DIRECT else "a3"
        arrived(kind, r, v[kind].at[r])
        mine = rows(xl * 64 + y * 16, 16)
        total = v["paf"][r, mine, :]
        for j in range(3 if r in DIRECT else 2):
            total = total + v[kind][r, j].astype(F32)
        v["hid"][r, mine, :CA] = jnp.maximum(total + v["ubias"][:, :CA], 0.0).astype(BF16)
        here = v["hid"].at[r, mine, pl.ds(0, CA)]
        if r in DIRECT:
            for j in (0, 2, 1):
                send("a3d", r, here, here, in_row[j])
        else:
            send("a4", r, here, here, above)
            send("a4", r, here, here, below)

    def s4b(r):
        arrived("b3", r, v["b3"].at[r])
        mine = rows(y * 32 + xl * 16, 16)
        total = v["pbf"][r, mine, :] + v["b3"][r].astype(F32)
        v["hid"][r, mine, CA:] = jnp.maximum(total + v["ubias"][:, CA:], 0.0).astype(BF16)
        here = v["hid"].at[r, mine, pl.ds(CA, CB)]
        send("b4", r, here, here, x_other)

    def s5a(r):
        arrived("a4", r, v["a3"].at[r])
        here = v["hid"].at[r, rows(xl * 64 + y_dn * 16, 16), pl.ds(0, HA)]
        send("a5", r, here, here, above)
        here = v["hid"].at[r, rows(xl * 64 + y_up * 16, 16), pl.ds(HA, HA)]
        send("a5", r, here, here, below)

    def y_back(r):
        arrived("b4", r, v["b3"].at[r])
        here = v["hid"].at[r, rows(y * 32, 32), pl.ds(CA, CB)]
        if r in DIRECT:
            for j in (0, 2, 1):
                send("b4d", r, here, here, in_row[j])
        else:
            send("b5", r, here, here, above)
            send("b5", r, here, here, below)

    def s5b(r):
        y_back(r)

    def s6a(r):
        if r in DIRECT:
            arrived("a3d", r, v["a2d"].at[r])
        else:
            arrived("a5", r, v["a2"].at[r])
        here = v["hid"].at[r, rows(xl * 64, 64), pl.ds(0, CA)]
        send("a6", r, here, here, x_other)

    def s6b(r):
        if r in DIRECT:
            y_back(r)
            return
        arrived("b5", r, v["b2"].at[r])
        here = v["hid"].at[r, rows(y_dn * 32, 16), pl.ds(CA, CB)]
        send("b6", r, here, here, above)
        here = v["hid"].at[r, rows(y_up * 32 + 16, 16), pl.ds(CA, CB)]
        send("b6", r, here, here, below)

    def g2(r):
        arrived("a6", r, v["a1"].at[r])
        if r in DIRECT:
            arrived("b4d", r, v["b1d"].at[r])
        else:
            arrived("b6", r, v["b1"].at[r])
        for n in range(0, W, 256):
            v["pf"][r, :, n:n + 256] = jnp.dot(v["hid"][r], v["wdn"][:, n:n + 256], preferred_element_type=F32)
        v["so"][r] = v["pf"][r, rows((1 - c) * 64, 64), :].astype(BF16)
        send("so", r, v["so"].at[r], v["sib"].at[r], sibling)

    def chip_sum(r, h):
        return v["pf"][r, rows(c * 64 + h * PIECE, PIECE), :] + v["sib"][r, h * PIECE:(h + 1) * PIECE].astype(F32)

    summed = set()

    def z_sum(r, h):
        if r not in summed:
            arrived("so", r, v["sib"].at[r])
            summed.add(r)
        part = pl.ds(h * PIECE, PIECE)
        total = chip_sum(r, h)
        if r in (1, 2, 6, 7) or (r == 3 and h < CUTS // 2) or (r == 5 and h >= CUTS // 2):
            arrived("zr", r * CUTS + h, v["zr"].at[r, part])
            total = total + v["zr"][r, part].astype(F32)
        v["zs"][r, part] = total.astype(BF16)
        step = -1 if r < 4 or (r == 4 and h < CUTS // 2) else 1
        there = (r + step) % N
        there = 4 if there == 0 and step > 0 else there
        send("zr", there * CUTS + h, v["zs"].at[r, part], v["zr"].at[there, part], ahead if step < 0 else behind)

    def finish(h):
        if 0 not in summed:
            arrived("so", 0, v["sib"].at[0])
            summed.add(0)
        part = pl.ds(h * PIECE, PIECE)
        arrived("zr", h, v["zr"].at[0, part])
        arrived("zr", 4 * CUTS + h, v["zr"].at[4, part])
        mixed = chip_sum(0, h) + v["zr"][0, part].astype(F32) + v["zr"][4, part].astype(F32)
        out[0, h * PIECE:(h + 1) * PIECE] = (v["xres"][h * PIECE:(h + 1) * PIECE] + mixed + v["dbias"][...]).astype(BF16)

    first_down = True
    chunk_steps = dict(
        g1=g1, s2a=s2a, s2b=s2b, s3a=s3a, s3b=s3b, s4a=s4a, s4b=s4b, s5a=s5a, s5b=s5b, s6a=s6a, s6b=s6b, g2=g2
    )
    first_up = True
    for name, r, h in ORDER:
        if name == "g1" and first_up:
            loads[5].wait()
            first_up = False
        if name == "g2" and first_down:
            loads[6].wait()
            first_down = False
        if name == "ga":
            ga(r, h)
        elif name == "n":
            normalize(h)
        elif name == "z" and r == 0:
            finish(h)
        elif name == "z":
            z_sum(r, h)
        else:
            chunk_steps[name](r)

    sent = dict(
        hand=v["hs"], agc=v["zr"], agz=v["zr"].at[pl.ds(0, 7)], a1=v["a1"], a6=v["a1"], b3=v["b3"], b4=v["b3"],
        so=v["sib"], zr=v["zr"].at[pl.ds(0, 7)],
    )
    by_ring = pl.ds(0, N - len(DIRECT))
    for kind, like in dict(a2="a2", a3="a3", b1="b1", b2="b2", a4="a3", a5="a2", b5="b2", b6="b1").items():
        if len(DIRECT) < N:
            sent[kind] = v[like].at[by_ring]
    for kind, like in dict(a2d="a2d", b1d="b1d", a3d="a2d", b4d="b1d").items():
        if DIRECT:
            sent[kind] = v[like].at[pl.ds(0, len(DIRECT))]
    for kind, like in sent.items():
        pltpu.make_async_copy(like, like, send_sem.at[SENDS.index(kind)]).wait()


def body(handoff, ln_gain, ln_bias, w_up, up_bias, w_down, down_bias):
    return pl.pallas_call(
        kernel,
        out_shape=jax.ShapeDtypeStruct((1, 64, W), BF16),
        in_specs=[pl.BlockSpec(memory_space=pl.ANY)] * 7,
        out_specs=pl.BlockSpec(memory_space=pltpu.VMEM),
        scratch_shapes=[pltpu.VMEM(shape, dtype) for shape, dtype in SCRATCH.values()] + [
            pltpu.SemaphoreType.DMA((7,)),
            pltpu.SemaphoreType.DMA((4,)),
            pltpu.SemaphoreType.DMA((len(SENDS),)),
            pltpu.SemaphoreType.DMA((LANDINGS,)),
        ],
        compiler_params=pltpu.CompilerParams(
            collective_id=0, has_side_effects=True, vmem_limit_bytes=60 << 20
        ),
        name="relay_block",
    )(handoff, ln_gain, ln_bias, w_up, up_bias, w_down, down_bias)


def solution(mesh):
    placed = (
        P("section", ("mp", "dp"), None),
        P("section", "dp"),
        P("section", "dp"),
        P("section", "dp", "mp"),
        P("section", "mp"),
        P("section", "mp", "dp"),
        P("section", "dp"),
    )
    return jax.shard_map(
        body, mesh=mesh, in_specs=placed, out_specs=P("section", "mp", "dp"), check_vma=False
    )
```

```python
import types

import jax
import jax.numpy as jnp
from jax import lax
from jax.experimental import pallas as pl
from jax.experimental.pallas import tpu as pltpu
from jax.sharding import PartitionSpec as P

D = 12288
W = 1536
N = 8
CA = 768
CB = W - CA
HA = CA // 2
CUTS = 4
PIECE = 64 // CUTS
DIRECT = ()
F32 = jnp.float32
BF16 = jnp.bfloat16
MESH = pl.DeviceIdType.MESH

N_, GA_, G1_, S2A_, S2B_, S3A_, S3B_, S4A_, S4B_, S5A_, S5B_, S6A_, S6B_, G2_, Z_ = range(15)
ORDER = (
    (N_, 0, 0), (N_, 0, 1), (N_, 0, 2), (N_, 0, 3), (GA_, 1, 0), (GA_, 7, 0), (GA_, 1, 1), (GA_, 7, 1), (G1_, 0, 0),
    (GA_, 1, 2), (GA_, 7, 2), (GA_, 7, 3), (GA_, 1, 3), (GA_, 6, 0), (GA_, 2, 0), (G1_, 7, 0), (GA_, 2, 1),
    (G1_, 1, 0), (GA_, 6, 1), (S2A_, 0, 0), (GA_, 2, 2), (S2B_, 0, 0), (GA_, 2, 3), (GA_, 6, 2), (GA_, 6, 3),
    (GA_, 5, 0), (S2B_, 7, 0), (G1_, 2, 0), (G1_, 6, 0), (GA_, 3, 2), (S2A_, 7, 0), (GA_, 3, 1), (GA_, 5, 1),
    (S2B_, 1, 0), (GA_, 3, 0), (GA_, 3, 3), (S2A_, 1, 0), (GA_, 5, 3), (GA_, 5, 2), (S3A_, 0, 0), (S2B_, 2, 0),
    (G1_, 3, 0), (GA_, 4, 0), (G1_, 5, 0), (GA_, 4, 2), (S2B_, 6, 0), (S2A_, 2, 0), (S3A_, 7, 0), (GA_, 4, 1),
    (GA_, 4, 3), (G1_, 4, 0), (S2B_, 3, 0), (S3B_, 0, 0), (S2A_, 3, 0), (S3A_, 1, 0), (S2A_, 6, 0), (S3A_, 2, 0),
    (S3B_, 7, 0), (S2B_, 4, 0), (S3B_, 2, 0), (S3B_, 1, 0), (S3B_, 3, 0), (S3A_, 3, 0), (S2A_, 4, 0), (S2B_, 5, 0),
    (S2A_, 5, 0), (S4A_, 1, 0), (S4B_, 7, 0), (S3B_, 4, 0), (S4B_, 1, 0), (S4A_, 3, 0), (S4B_, 0, 0), (S4B_, 3, 0),
    (S3A_, 4, 0), (S4A_, 7, 0), (S3A_, 6, 0), (S3B_, 5, 0), (S3A_, 5, 0), (S4A_, 2, 0), (S4B_, 4, 0), (S4B_, 2, 0),
    (S5A_, 3, 0), (S3B_, 6, 0), (S4A_, 4, 0), (S5B_, 3, 0), (S4A_, 5, 0), (S5B_, 4, 0), (S4B_, 5, 0), (S4B_, 6, 0),
    (S5A_, 4, 0), (S4A_, 6, 0), (S6A_, 3, 0), (S6B_, 3, 0), (S5A_, 5, 0), (S5B_, 5, 0), (S6B_, 4, 0), (S5A_, 2, 0),
    (S6A_, 4, 0), (S5A_, 7, 0), (S5B_, 2, 0), (S5A_, 6, 0), (S5B_, 6, 0), (S6A_, 5, 0), (S5A_, 1, 0), (G2_, 3, 0),
    (S6B_, 5, 0), (S6A_, 2, 0), (G2_, 4, 0), (Z_, 3, 2), (S5B_, 1, 0), (S6A_, 6, 0), (S6B_, 2, 0), (S5B_, 7, 0),
    (S6A_, 1, 0), (Z_, 4, 0), (Z_, 4, 2), (G2_, 5, 0), (S6B_, 6, 0), (Z_, 4, 3), (Z_, 4, 1), (S4A_, 0, 0), (Z_, 3, 3),
    (Z_, 5, 0), (Z_, 5, 1), (G2_, 2, 0), (S6A_, 7, 0), (Z_, 3, 0), (Z_, 5, 2), (S6B_, 1, 0), (S6B_, 7, 0),
    (S5B_, 0, 0), (G2_, 6, 0), (Z_, 5, 3), (Z_, 3, 1), (S5A_, 0, 0), (Z_, 2, 2), (Z_, 6, 0), (Z_, 2, 3), (G2_, 1, 0),
    (Z_, 6, 1), (Z_, 6, 2), (Z_, 2, 0), (G2_, 7, 0), (Z_, 6, 3), (Z_, 2, 1), (Z_, 1, 2), (S6A_, 0, 0), (S6B_, 0, 0),
    (Z_, 7, 0), (Z_, 1, 3), (Z_, 7, 1), (Z_, 7, 2), (Z_, 1, 0), (Z_, 7, 3), (Z_, 1, 1), (G2_, 0, 0), (Z_, 0, 1),
    (Z_, 0, 0), (Z_, 0, 2), (Z_, 0, 3),
)

SCRATCH = dict(
    hand=((8, D), BF16),
    wup=((W, W), BF16),
    wdn=((W, W), BF16),
    gain=((1, W), F32),
    bias=((1, W), F32),
    ubias=((1, W), F32),
    dbias=((1, W), F32),
    hs=((8, 16, 896), BF16),
    hr=((8, 16, 896), BF16),
    xres=((64, W), F32),
    nrm=((N, 128, W), BF16),
    paf=((N, 128, CA), F32),
    pbf=((N, 128, CB), F32),
    pab=((N, 128, CA), BF16),
    pbb=((N, 128, CB), BF16),
    a1=((N, 64, CA), BF16),
    a2=((N, 2, 16, HA), BF16),
    a3=((N, 2, 16, CA), BF16),
    a2d=((N, 3, 16, CA), BF16),
    b1=((N, 2, 16, CB), BF16),
    b2=((N, 2, 32, CB), BF16),
    b1d=((N, 3, 32, CB), BF16),
    b3=((N, 16, CB), BF16),
    sa=((N, 64, CA), BF16),
    sa2=((N, 2, 16, CA), BF16),
    sb2=((N, 2, 32, CB), BF16),
    sb=((N, 16, CB), BF16),
    hid=((N, 128, W), BF16),
    pf=((N, 128, W), F32),
    so=((N, 64, W), BF16),
    sib=((N, 64, W), BF16),
    zs=((N, 64, W), BF16),
    zr=((N, 64, W), BF16),
)
KINDS = (
    "agc", "agz", "a1", "a2", "a3", "a2d", "b1", "b2", "b1d", "b3",
    "a4", "a5", "a3d", "a6", "b4", "b5", "b6", "b4d", "so", "zr",
)
SENDS = ("hand",) + KINDS
LANDINGS = 168


def kernel(hand_in, gain_in, bias_in, wup_in, ubias_in, wdn_in, dbias_in, out, *refs):
    named = dict(zip(SCRATCH, refs))
    v = types.SimpleNamespace(**named)
    local_sem, hand_sem, send_sem, recv_sem = refs[len(SCRATCH):]
    s = lax.axis_index("section")
    d = lax.axis_index("dp")
    m = lax.axis_index("mp")
    xl, y, z, c = d // 4, d % 4, m // 2, m % 2
    other_y = [(y + j) % 4 for j in (1, 2, 3)]
    z_up, z_dn = (z + 1) % N, (z + N - 1) % N

    def at(section=s, x=xl, row=y, deep=z, core=c):
        return (section, x * 4 + row, deep * 2 + core)

    sibling = at(core=1 - c)
    x_other = at(x=1 - xl)
    in_row = [at(row=row) for row in other_y]
    y_up, y_far, y_dn = other_y
    above, below = in_row[0], in_row[2]
    ahead, behind = at(deep=z_up), at(deep=z_dn)

    loads = []
    for i, (src, dst) in enumerate((
        (hand_in, "hand"), (gain_in, None), (bias_in, None), (ubias_in, None), (dbias_in, None),
        (wup_in, "wup"), (wdn_in, "wdn"),
    )):
        name = ("hand", "gain", "bias", "ubias", "dbias", "wup", "wdn")[i]
        from_ref = src.at[0] if dst else src
        load = pltpu.make_async_copy(from_ref, named[name], local_sem.at[i])
        load.start()
        loads.append(load)

    barrier = pltpu.get_barrier_semaphore()
    others = [(1 - s, i, m) for i in range(8)]
    near = [sibling, x_other, *in_row, ahead, behind]
    for device in others + near:
        pl.semaphore_signal(barrier, inc=1, device_id=device, device_id_type=MESH)

    slots = {}

    def landed(kind, k):
        return recv_sem.at[slots.setdefault((kind, k), len(slots))]

    def send(kind, k, src, dst, device):
        pltpu.make_async_remote_copy(
            src_ref=src,
            dst_ref=dst,
            send_sem=send_sem.at[SENDS.index(kind)],
            recv_sem=landed(kind, k),
            device_id=device,
            device_id_type=MESH,
        ).start()

    def arrived(kind, k, like):
        pltpu.make_async_copy(like, like, landed(kind, k)).wait()

    def rows(start, size):
        return pl.ds(pl.multiple_of(start, 16), size)

    loads[0].wait()
    x = v.hand[...].astype(F32)
    mean = jnp.sum(x, axis=1, keepdims=True) / D
    centred = x - mean
    rstd = lax.rsqrt(jnp.sum(centred * centred, axis=1, keepdims=True) / D + 1e-05)
    lane = lax.broadcasted_iota(jnp.int32, (8, 128), 1)

    def parts(value):
        high = value.astype(BF16).astype(F32)
        rest = value - high
        middle = rest.astype(BF16).astype(F32)
        low = rest - middle
        return jnp.where(lane < 32, high, jnp.where(lane < 64, middle, low))

    stats = jnp.concatenate([parts(mean), parts(rstd)], axis=0).astype(BF16)
    for i in range(8):
        left = x[:, i * W:i * W + 768]
        right = x[:, i * W + 768:(i + 1) * W]
        v.hs[i, :, :768] = jnp.concatenate([left, right], axis=0).astype(BF16)
        v.hs[i, :, 768:] = stats
    pl.semaphore_wait(barrier, len(others) + len(near))
    def partner(step):
        low = 1 - d % 2 if step % 2 else d % 2
        return (d // 2 + step // 2) % 4 * 2 + low

    for i in range(8):
        other = partner(i)
        pltpu.make_async_remote_copy(
            src_ref=v.hs.at[other],
            dst_ref=v.hr.at[d],
            send_sem=send_sem.at[0],
            recv_sem=hand_sem.at[i // 2],
            device_id=(1 - s, other, m),
            device_id_type=MESH,
        ).start()
    for load in loads[1:5]:
        load.wait()

    def piece(p):
        return (d // 2 + 4 - p) % 4 * 16

    def unpack(i):
        held = v.hr[i].astype(F32)
        stat = held[:, 768:]
        stat = stat[:, 0:1] + stat[:, 32:33] + stat[:, 64:65]
        return jnp.concatenate([held[:8, :768], held[8:, :768]], axis=1), stat[:8], stat[8:]

    def block(r, p):
        return v.nrm.at[(z + r) % N, rows(c * 64 + piece(p), 16)]

    def pair(r, p):
        send("agc", r % N, block(r, p), block(r, p), sibling)

    def ring(r, h, step):
        send("agz", (r + step) % N * CUTS + h, block(r, h), block(r, h), ahead if step < 0 else behind)

    def normalize(p):
        pltpu.make_async_copy(v.hr.at[pl.ds(0, 2)], v.hr.at[pl.ds(0, 2)], hand_sem.at[p]).wait()
        first = piece(p) // 8
        xa, mean_a, rstd_a = unpack(first)
        xb, mean_b, rstd_b = unpack(first + 1)
        two = jnp.concatenate([(xa - mean_a) * rstd_a, (xb - mean_b) * rstd_b], axis=0)
        v.nrm[z, rows(c * 64 + piece(p), 16), :] = (two * v.gain[...] + v.bias[...]).astype(BF16)
        v.xres[rows(piece(p), 16), :] = jnp.concatenate([xa, xb], axis=0)
        ring(0, p, -1)
        ring(0, p, 1)
        pair(0, p)

    def ga(r, h):
        arrived("agz", r * CUTS + h, v.zr.at[0, pl.ds(0, PIECE)])
        step = -1 if r > 4 else 1
        if r != 4 and (r + step != 4 or (h < CUTS // 2) == (step < 0)):
            ring(r, h, step)
        pair(r, h)

    def g1(r):
        own = (z + r) % N
        arrived("agc", r, v.zr.at[0])
        for n in range(0, W, 256):
            part = jnp.dot(v.nrm[own], v.wup[:, n:n + 256], preferred_element_type=F32)
            f, b, first = ("paf", "pab", n) if n < CA else ("pbf", "pbb", n - CA)
            named[f][r, :, first:first + 256] = part
            named[b][r, :, first:first + 256] = part.astype(BF16)
        send("a1", r, v.pab.at[r, rows((1 - xl) * 64, 64)], v.a1.at[r], x_other)
        if r in DIRECT:
            for j in (0, 2, 1):
                send("b1d", r, v.pbb.at[r, rows(other_y[j] * 32, 32)], v.b1d.at[r, j], in_row[j])
        else:
            send("b1", r, v.pbb.at[r, rows(y_far * 32, 16)], v.b1.at[r, 0], above)
            send("b1", r, v.pbb.at[r, rows(y_far * 32 + 16, 16)], v.b1.at[r, 1], below)

    def s2a(r):
        arrived("a1", r, v.a1.at[r])
        total = v.paf[r, rows(xl * 64, 64), :] + v.a1[r].astype(F32)
        v.paf[r, rows(xl * 64, 64), :] = total
        v.sa[r] = total.astype(BF16)
        if r in DIRECT:
            for j in (0, 2, 1):
                send("a2d", r, v.sa.at[r, rows(other_y[j] * 16, 16)], v.a2d.at[r, j], in_row[j])
        else:
            far = rows(y_far * 16, 16)
            send("a2", r, v.sa.at[r, far, pl.ds(0, HA)], v.a2.at[r, 0], above)
            send("a2", r, v.sa.at[r, far, pl.ds(HA, HA)], v.a2.at[r, 1], below)

    def x_sums(r, kind):
        def total(x):
            sums = v.pbf[r, rows(y * 32 + x * 16, 16), :]
            for j in range(3 if kind == "b1d" else 2):
                sums = sums + named[kind][r, j, rows(x * 16, 16), :].astype(F32)
            return sums

        v.sb[r] = total(1 - xl).astype(BF16)
        send("b3", r, v.sb.at[r], v.b3.at[r], x_other)
        v.pbf[r, rows(y * 32 + xl * 16, 16), :] = total(xl)

    def s2b(r):
        if r in DIRECT:
            arrived("b1d", r, v.b1d.at[r])
            x_sums(r, "b1d")
            return
        arrived("b1", r, v.b1.at[r])
        up, down = rows(y_up * 32, 16), rows(y_dn * 32 + 16, 16)
        v.sb2[r, 0, :16] = (v.pbf[r, up, :] + v.b1[r, 0].astype(F32)).astype(BF16)
        v.sb2[r, 0, 16:] = v.pbb[r, rows(y_up * 32 + 16, 16), :]
        send("b2", r, v.sb2.at[r, 0], v.b2.at[r, 0], above)
        v.sb2[r, 1, :16] = v.pbb[r, rows(y_dn * 32, 16), :]
        v.sb2[r, 1, 16:] = (v.pbf[r, down, :] + v.b1[r, 1].astype(F32)).astype(BF16)
        send("b2", r, v.sb2.at[r, 1], v.b2.at[r, 1], below)

    def s3a(r):
        arrived("a2", r, v.a2.at[r])
        up = v.paf[r, rows(xl * 64 + y_up * 16, 16), :]
        v.sa2[r, 0, :, :HA] = (up[:, :HA] + v.a2[r, 0].astype(F32)).astype(BF16)
        v.sa2[r, 0, :, HA:] = up[:, HA:].astype(BF16)
        send("a3", r, v.sa2.at[r, 0], v.a3.at[r, 0], above)
        down = v.paf[r, rows(xl * 64 + y_dn * 16, 16), :]
        v.sa2[r, 1, :, :HA] = down[:, :HA].astype(BF16)
        v.sa2[r, 1, :, HA:] = (down[:, HA:] + v.a2[r, 1].astype(F32)).astype(BF16)
        send("a3", r, v.sa2.at[r, 1], v.a3.at[r, 1], below)

    def s3b(r):
        arrived("b2", r, v.b2.at[r])
        x_sums(r, "b2")

    def s4a(r):
        kind = "a2d" if r in DIRECT else "a3"
        arrived(kind, r, named[kind].at[r])
        mine = rows(xl * 64 + y * 16, 16)
        total = v.paf[r, mine, :]
        for j in range(3 if r in DIRECT else 2):
            total = total + named[kind][r, j].astype(F32)
        v.hid[r, mine, :CA] = jnp.maximum(total + v.ubias[:, :CA], 0.0).astype(BF16)
        here = v.hid.at[r, mine, pl.ds(0, CA)]
        if r in DIRECT:
            for j in (0, 2, 1):
                send("a3d", r, here, here, in_row[j])
        else:
            send("a4", r, here, here, above)
            send("a4", r, here, here, below)

    def s4b(r):
        arrived("b3", r, v.b3.at[r])
        mine = rows(y * 32 + xl * 16, 16)
        total = v.pbf[r, mine, :] + v.b3[r].astype(F32)
        v.hid[r, mine, CA:] = jnp.maximum(total + v.ubias[:, CA:], 0.0).astype(BF16)
        here = v.hid.at[r, mine, pl.ds(CA, CB)]
        send("b4", r, here, here, x_other)

    def s5a(r):
        arrived("a4", r, v.a3.at[r])
        here = v.hid.at[r, rows(xl * 64 + y_dn * 16, 16), pl.ds(0, HA)]
        send("a5", r, here, here, above)
        here = v.hid.at[r, rows(xl * 64 + y_up * 16, 16), pl.ds(HA, HA)]
        send("a5", r, here, here, below)

    def y_back(r):
        arrived("b4", r, v.b3.at[r])
        here = v.hid.at[r, rows(y * 32, 32), pl.ds(CA, CB)]
        if r in DIRECT:
            for j in (0, 2, 1):
                send("b4d", r, here, here, in_row[j])
        else:
            send("b5", r, here, here, above)
            send("b5", r, here, here, below)

    def s5b(r):
        y_back(r)

    def s6a(r):
        if r in DIRECT:
            arrived("a3d", r, v.a2d.at[r])
        else:
            arrived("a5", r, v.a2.at[r])
        here = v.hid.at[r, rows(xl * 64, 64), pl.ds(0, CA)]
        send("a6", r, here, here, x_other)

    def s6b(r):
        if r in DIRECT:
            y_back(r)
            return
        arrived("b5", r, v.b2.at[r])
        here = v.hid.at[r, rows(y_dn * 32, 16), pl.ds(CA, CB)]
        send("b6", r, here, here, above)
        here = v.hid.at[r, rows(y_up * 32 + 16, 16), pl.ds(CA, CB)]
        send("b6", r, here, here, below)

    def g2(r):
        arrived("a6", r, v.a1.at[r])
        if r in DIRECT:
            arrived("b4d", r, v.b1d.at[r])
        else:
            arrived("b6", r, v.b1.at[r])
        for n in range(0, W, 256):
            v.pf[r, :, n:n + 256] = jnp.dot(v.hid[r], v.wdn[:, n:n + 256], preferred_element_type=F32)
        v.so[r] = v.pf[r, rows((1 - c) * 64, 64), :].astype(BF16)
        send("so", r, v.so.at[r], v.sib.at[r], sibling)

    def chip_sum(r, h):
        return v.pf[r, rows(c * 64 + h * PIECE, PIECE), :] + v.sib[r, h * PIECE:(h + 1) * PIECE].astype(F32)

    summed = set()

    def z_sum(r, h):
        if r not in summed:
            arrived("so", r, v.sib.at[r])
            summed.add(r)
        part = pl.ds(h * PIECE, PIECE)
        total = chip_sum(r, h)
        if r in (1, 2, 6, 7) or (r == 3 and h < CUTS // 2) or (r == 5 and h >= CUTS // 2):
            arrived("zr", r * CUTS + h, v.zr.at[r, part])
            total = total + v.zr[r, part].astype(F32)
        v.zs[r, part] = total.astype(BF16)
        step = -1 if r < 4 or (r == 4 and h < CUTS // 2) else 1
        there = (r + step) % N
        there = 4 if there == 0 and step > 0 else there
        send("zr", there * CUTS + h, v.zs.at[r, part], v.zr.at[there, part], ahead if step < 0 else behind)

    def finish(h):
        if 0 not in summed:
            arrived("so", 0, v.sib.at[0])
            summed.add(0)
        part = pl.ds(h * PIECE, PIECE)
        arrived("zr", h, v.zr.at[0, part])
        arrived("zr", 4 * CUTS + h, v.zr.at[4, part])
        mixed = chip_sum(0, h) + v.zr[0, part].astype(F32) + v.zr[4, part].astype(F32)
        out[0, h * PIECE:(h + 1) * PIECE] = (v.xres[h * PIECE:(h + 1) * PIECE] + mixed + v.dbias[...]).astype(BF16)

    first_down = True
    chunk_steps = {
        G1_: g1,
        S2A_: s2a,
        S2B_: s2b,
        S3A_: s3a,
        S3B_: s3b,
        S4A_: s4a,
        S4B_: s4b,
        S5A_: s5a,
        S5B_: s5b,
        S6A_: s6a,
        S6B_: s6b,
        G2_: g2,
    }
    first_up = True
    for name, r, h in ORDER:
        if name == G1_ and first_up:
            loads[5].wait()
            first_up = False
        if name == G2_ and first_down:
            loads[6].wait()
            first_down = False
        if name == GA_:
            ga(r, h)
        elif name == N_:
            normalize(h)
        elif name == Z_ and r == 0:
            finish(h)
        elif name == Z_:
            z_sum(r, h)
        else:
            chunk_steps[name](r)

    sent = dict(
        hand=v.hs, agc=v.zr, agz=v.zr.at[pl.ds(0, 7)], a1=v.a1, a6=v.a1, b3=v.b3, b4=v.b3,
        so=v.sib, zr=v.zr.at[pl.ds(0, 7)],
    )
    by_ring = pl.ds(0, N - len(DIRECT))
    for kind, like in dict(a2="a2", a3="a3", b1="b1", b2="b2", a4="a3", a5="a2", b5="b2", b6="b1").items():
        if len(DIRECT) < N:
            sent[kind] = named[like].at[by_ring]
    for kind, like in dict(a2d="a2d", b1d="b1d", a3d="a2d", b4d="b1d").items():
        if DIRECT:
            sent[kind] = named[like].at[pl.ds(0, len(DIRECT))]
    for kind, like in sent.items():
        pltpu.make_async_copy(like, like, send_sem.at[SENDS.index(kind)]).wait()


def body(handoff, ln_gain, ln_bias, w_up, up_bias, w_down, down_bias):
    return pl.pallas_call(
        kernel,
        out_shape=jax.ShapeDtypeStruct((1, 64, W), BF16),
        in_specs=[pl.BlockSpec(memory_space=pl.ANY)] * 7,
        out_specs=pl.BlockSpec(memory_space=pltpu.VMEM),
        scratch_shapes=[pltpu.VMEM(shape, dtype) for shape, dtype in SCRATCH.values()] + [
            pltpu.SemaphoreType.DMA((7,)),
            pltpu.SemaphoreType.DMA((4,)),
            pltpu.SemaphoreType.DMA((len(SENDS),)),
            pltpu.SemaphoreType.DMA((LANDINGS,)),
        ],
        compiler_params=pltpu.CompilerParams(
            collective_id=0, has_side_effects=True, vmem_limit_bytes=60 << 20
        ),
        name="relay_block",
    )(handoff, ln_gain, ln_bias, w_up, up_bias, w_down, down_bias)


def solution(mesh):
    placed = (
        P("section", ("mp", "dp"), None),
        P("section", "dp"),
        P("section", "dp"),
        P("section", "dp", "mp"),
        P("section", "mp"),
        P("section", "mp", "dp"),
        P("section", "dp"),
    )
    return jax.shard_map(
        body, mesh=mesh, in_specs=placed, out_specs=P("section", "mp", "dp"), check_vma=False
    )
```
